32 devices in a mesh: grp: 4 (over x, core), tile: 8 (over z, y).
Axes of the slice: x: 2, y: 2, z: 4, core: 2. Of those that a mesh axis runs over, the one named last changes fastest.
Arguments:
- height_model: float32 [4608, 1024], P('grp', 'tile'), as said below
- scenario_trigger_indicator: int32 [4, 256, 512], P('grp', 'tile'), may hold values 0 or 1
- initial_snow_thickness_cm: int32 [4, 256, 512], P('grp', 'tile'), may hold values from 20 to 300
- frame_leading_northing_index: int32 [4], P('grp'), may hold values from 3 to 4349
- frame_leading_easting_index: int32 [4], P('grp'), may hold values from 3 to 509
Outputs:
- ground_geometry: float32 [4, 4608, 1024], P(None, 'grp', 'tile')
- flow: float32 [4, 3, 256, 512], P('grp', None, 'tile')
The draws below stay inside these ranges and needn't reach their ends.
Inputs may be any that keep to these rules, and one draw needn't show every extreme that they name: `frame_leading_northing_index`: each window, widened by 3 cells on every side, lies inside the DEM rows. `frame_leading_easting_index`: each window, widened by 3 cells on every side, lies inside the DEM columns. `height_model`: elevation in metres, near zero at the DEM's rim within a few metres.
All inputs are finite; a program needn't handle non-finite values. No bound on the sum of `scenario_trigger_indicator` on one device may be relied on, other than what follows from the above.
Results may differ from the reference program's by a relative error of at most 0.0003.
Values sent between devices are 32-bit elements; how exact they have to be, the bound alone decides.
A program may use at most 64 MiB of HBM per device.

```python
import math
import jax
import jax.numpy as jnp
from jax import lax

KERNEL_SPAN = 3
STEPS = 4
NR = 4608
NC = 1024
WR = 256
WC = 512
SCEN = 4


def draw_height_model(key, part):
    row_pos = (jnp.arange(NR, dtype=jnp.float32) + 0.5) / NR
    col_pos = (jnp.arange(NC, dtype=jnp.float32) + 0.5) / NC
    phase_key = jax.random.fold_in(key, 11)
    noise_key = jax.random.fold_in(key, 23)
    phase = jax.random.uniform(phase_key, (), jnp.float32, -math.pi, math.pi)
    dome = jnp.sin(math.pi * row_pos)[:, None] * jnp.sin(math.pi * col_pos)[None, :]
    ridges = jnp.cos(2.0 * math.pi * (7.0 * row_pos[:, None] + 13.0 * col_pos[None, :]) + phase)
    rough = 0.5 * jax.random.normal(noise_key, (NR, NC), jnp.float32)
    return dome * (300.0 + 150.0 * ridges) + rough


def plant(entries, stream_key, smallest, top_value):
    extent = entries.shape
    index_at = [jax.random.randint(jax.random.fold_in(stream_key, axis), (), 0, extent[axis]) for axis in range(len(extent))]
    entries = entries.at[tuple(index_at)].set(smallest)
    longest = extent.index(max(extent))
    index_at[longest] = (index_at[longest] + 1) % extent[longest]
    return entries.at[tuple(index_at)].set(top_value)


def setup_inputs(seed: int = 0) -> dict:
    seeds = jax.random.split(jax.random.key(seed), 6)
    return {
        "height_model": draw_height_model(jax.random.fold_in(seeds[5], 71), 0),
        "scenario_trigger_indicator": plant((jax.random.randint(seeds[1], (SCEN, WR, WC), 0, 2) < 1).astype(jnp.int32), jax.random.fold_in(seeds[1], 1), 0, 1),
        "initial_snow_thickness_cm": plant(jax.random.randint(seeds[2], (SCEN, WR, WC), 20, 301), jax.random.fold_in(seeds[2], 1), 20, 300).astype(jnp.int32),
        "frame_leading_northing_index": plant(jax.random.randint(seeds[3], (SCEN,), KERNEL_SPAN, NR - WR - KERNEL_SPAN + 1), jax.random.fold_in(seeds[3], 1), KERNEL_SPAN, NR - WR - KERNEL_SPAN).astype(jnp.int32),
        "frame_leading_easting_index": plant(jax.random.randint(seeds[4], (SCEN,), KERNEL_SPAN, NC - WC - KERNEL_SPAN + 1), jax.random.fold_in(seeds[4], 1), KERNEL_SPAN, NC - WC - KERNEL_SPAN).astype(jnp.int32),
    }


cell_size = 2.0
gravity = 9.81
time_step = 0.1
friction = 0.2
turbulence = 500.0
depth_floor = 0.1
speed_floor = 0.5
binomial = (0.0625, 0.25, 0.375, 0.25, 0.0625)

def derive_gradient_fields(framed_elevation_grid):
    inner_rows = framed_elevation_grid.shape[0] - 2 * KERNEL_SPAN
    inner_cols = framed_elevation_grid.shape[1] - 2 * KERNEL_SPAN
    across = binomial[0] * framed_elevation_grid[0:inner_rows + 2, :]
    for offset in range(1, 5):
        across = across + binomial[offset] * framed_elevation_grid[offset:offset + inner_rows + 2, :]
    smooth = binomial[0] * across[:, 0:inner_cols + 2]
    for offset in range(1, 5):
        smooth = smooth + binomial[offset] * across[:, offset:offset + inner_cols + 2]
    centre = smooth[1:-1, 1:-1]
    upper_cell = smooth[2:, 1:-1]
    lower_cell = smooth[:-2, 1:-1]
    right_cell = smooth[1:-1, 2:]
    left_cell = smooth[1:-1, :-2]
    grad_rows = (upper_cell - lower_cell) / (2.0 * cell_size)
    grad_cols = (right_cell - left_cell) / (2.0 * cell_size)
    curvature = (upper_cell + lower_cell + right_cell + left_cell - 4.0 * centre) / (cell_size * cell_size)
    upright = 1.0 / jnp.sqrt(1.0 + grad_rows * grad_rows + grad_cols * grad_cols)
    return jnp.stack([-grad_rows * upright, -grad_cols * upright, upright, curvature])

def advance(framed_elevation_grid, patch):
    depth_now = framed_elevation_grid[0]
    momentum_a = framed_elevation_grid[1]
    momentum_b = framed_elevation_grid[2]
    safe_depth = jnp.maximum(depth_now, depth_floor)
    velocity_a = momentum_a / safe_depth
    velocity_b = momentum_b / safe_depth
    wave_speed = jnp.sqrt(gravity * (jnp.maximum(depth_now, 0.0) + depth_floor))
    pressure = 0.5 * gravity * depth_now * depth_now
    flux_rows = jnp.stack([momentum_a, momentum_a * velocity_a + pressure, momentum_b * velocity_a])
    flux_cols = jnp.stack([momentum_b, momentum_a * velocity_b, momentum_b * velocity_b + pressure])
    reach_rows = jnp.abs(velocity_a) + wave_speed
    reach_cols = jnp.abs(velocity_b) + wave_speed
    bound_rows = jnp.maximum(reach_rows[:-1, 1:-1], reach_rows[1:, 1:-1])
    face_rows = 0.5 * (flux_rows[:, :-1, 1:-1] + flux_rows[:, 1:, 1:-1]) - 0.5 * bound_rows * (framed_elevation_grid[:, 1:, 1:-1] - framed_elevation_grid[:, :-1, 1:-1])
    bound_cols = jnp.maximum(reach_cols[1:-1, :-1], reach_cols[1:-1, 1:])
    face_cols = 0.5 * (flux_cols[:, 1:-1, :-1] + flux_cols[:, 1:-1, 1:]) - 0.5 * bound_cols * (framed_elevation_grid[:, 1:-1, 1:] - framed_elevation_grid[:, 1:-1, :-1])
    interior = framed_elevation_grid[:, 1:-1, 1:-1]
    updated = interior - time_step / cell_size * (face_rows[:, 1:] - face_rows[:, :-1] + face_cols[:, :, 1:] - face_cols[:, :, :-1])
    new_depth = updated[0]
    drive_a = updated[1] + time_step * gravity * interior[0] * patch[0]
    drive_b = updated[2] + time_step * gravity * interior[0] * patch[1]
    floor_depth = jnp.maximum(new_depth, depth_floor)
    rate_a = drive_a / floor_depth
    rate_b = drive_b / floor_depth
    square = rate_a * rate_a + rate_b * rate_b
    speed_norm = jnp.sqrt(square + speed_floor * speed_floor)
    normal_load = jnp.maximum(gravity * patch[2] + patch[3] * square, 0.0)
    drag_factor = time_step * (friction * normal_load / speed_norm + gravity * speed_norm / (turbulence * floor_depth))
    return jnp.stack([new_depth, drive_a / (1.0 + drag_factor), drive_b / (1.0 + drag_factor)])

def reference(height_model, scenario_trigger_indicator, initial_snow_thickness_cm, frame_leading_northing_index, frame_leading_easting_index):
    ground_geometry = derive_gradient_fields(jnp.pad(height_model, KERNEL_SPAN))
    results = []
    for scenario in range(SCEN):
        row_start = frame_leading_northing_index[scenario].astype(jnp.int32)
        col_start = frame_leading_easting_index[scenario].astype(jnp.int32)
        patch_terrain = lax.dynamic_slice(ground_geometry, (jnp.zeros((), jnp.int32), row_start, col_start), (4, WR, WC))
        release_depth = scenario_trigger_indicator[scenario].astype(jnp.float32) * initial_snow_thickness_cm[scenario].astype(jnp.float32) * 0.01
        empty_field = jnp.zeros_like(release_depth)
        flow_state = jnp.stack([release_depth, empty_field, empty_field])
        for turn_index in range(STEPS):
            flow_state = advance(jnp.pad(flow_state, ((0, 0), (1, 1), (1, 1))), patch_terrain)
        results.append(flow_state)
    return (ground_geometry, jnp.stack(results))
```

```python
import functools
import jax
import jax.numpy as jnp
from jax import lax
from jax.experimental import pallas as pl
from jax.experimental.pallas import tpu as pltpu
from jax.sharding import PartitionSpec as P

STEPS = 4
REACH = 3
LANES = 128
SUB = 8
PACKS = 16
CHUNK = 64

cell_size = 2.0
gravity = 9.81
time_step = 0.1
friction = 0.2
turbulence = 500.0
depth_floor = 0.1
speed_floor = 0.5
binomial = (0.0625, 0.25, 0.375, 0.25, 0.0625)
still_wave = (gravity * depth_floor) ** 0.5

MESH = pl.DeviceIdType.MESH


def shifted(x, by, axis):
    size = x.shape[axis]
    by = by % size
    return x if by == 0 else pltpu.roll(x, size - by, axis)


def five_taps(x, axis):
    outer = x + shifted(x, 4, axis)
    inner = shifted(x, 1, axis) + shifted(x, 3, axis)
    return binomial[0] * outer + binomial[1] * inner + binomial[2] * shifted(x, 2, axis)


def normal_fields(up, low, right, left, centre):
    grad_r = (up - low) * 0.25
    grad_c = (right - left) * 0.25
    curvature = (up + low + right + left - 4.0 * centre) * 0.25
    upright = lax.rsqrt(1.0 + grad_r * grad_r + grad_c * grad_c)
    return -grad_r * upright, -grad_c * upright, upright, curvature


def flow_step(state, patch, row_ok, col):
    depth, mom_r, mom_c = state
    n_r, n_c, n_z, kappa = patch
    width = depth.shape[1]
    inv = 1.0 / jnp.maximum(depth, depth_floor)
    u_r = mom_r * inv
    u_c = mom_c * inv
    wave = jnp.sqrt(gravity * (jnp.maximum(depth, 0.0) + depth_floor))
    pressure = 0.5 * gravity * depth * depth

    reach = jnp.abs(u_r) + wave
    bound = jnp.maximum(reach, shifted(reach, 1, 0))
    gains = []
    for q, f in (
        (depth, mom_r),
        (mom_r, mom_r * u_r + pressure),
        (mom_c, mom_c * u_r),
    ):
        face = (f + shifted(f, 1, 0)) - bound * (shifted(q, 1, 0) - q)
        gains.append(face - shifted(face, -1, 0))

    reach = jnp.abs(u_c) + wave
    last = col == width - 1
    first = col == 0
    bound = jnp.maximum(reach, jnp.where(last, still_wave, shifted(reach, 1, 1)))
    rim_bound = jnp.maximum(reach, still_wave)
    totals = []
    for gain, q, f in zip(
        gains,
        (depth, mom_r, mom_c),
        (mom_c, mom_r * u_c, mom_c * u_c + pressure),
    ):
        q_next = jnp.where(last, 0.0, shifted(q, 1, 1))
        f_next = jnp.where(last, 0.0, shifted(f, 1, 1))
        face = (f + f_next) - bound * (q_next - q)
        before = jnp.where(first, f - rim_bound * q, shifted(face, -1, 1))
        totals.append(gain + (face - before))

    scale = 0.5 * time_step / cell_size
    new_depth = depth - scale * totals[0]
    push = time_step * gravity * depth
    new_r = mom_r - scale * totals[1] + push * n_r
    new_c = mom_c - scale * totals[2] + push * n_c
    inv = 1.0 / jnp.maximum(new_depth, depth_floor)
    v_r = new_r * inv
    v_c = new_c * inv
    square = v_r * v_r + v_c * v_c
    energy = square + speed_floor * speed_floor
    inv_speed = lax.rsqrt(energy)
    load = jnp.maximum(gravity * n_z + kappa * square, 0.0)
    drag = time_step * (
        friction * load * inv_speed + (gravity / turbulence) * (energy * inv_speed) * inv
    )
    damp = 1.0 / (1.0 + drag)
    return (
        jnp.where(row_ok, new_depth, 0.0),
        jnp.where(row_ok, new_r * damp, 0.0),
        jnp.where(row_ok, new_c * damp, 0.0),
    )


def kernel(
    groups,
    tiles,
    north_ref,
    east_ref,
    trigger_ref,
    snow_ref,
    height_ref,
    geo_out,
    flow_out,
    high,
    side,
    smooth,
    diff_c,
    sum_c,
    geo,
    packed,
    packed_in,
    edge_in,
    depth_own,
    depth_in,
    index,
    strip_out,
    strip_in,
    strip,
    block_in,
    state,
    load_sem,
    store_sem,
    send_sem,
    recv_sem,
    strip_send,
    strip_recv,
    block_send,
    block_recv,
):
    g = lax.axis_index("grp")
    t = lax.axis_index("tile")
    rows = height_ref.shape[0]
    piece = trigger_ref.shape[1]
    width = trigger_ref.shape[2]
    span = strip.shape[0]
    block_rows = block_in.shape[1]
    window_rows = piece * tiles
    pad = span
    state_rows = piece + 2 * STEPS
    north_of = lambda d: lax.rem(g + d + groups, groups)
    east_of = lambda d: lax.rem(t + d + tiles, tiles)

    load = pltpu.make_async_copy(height_ref, high.at[pl.ds(pad, rows)], load_sem)
    load.start()

    barrier = pltpu.get_barrier_semaphore()
    peers = (
        [(north_of(d), t) for d in range(1, groups)]
        + [(g, east_of(d)) for d in range(1, tiles)]
        + [(north_of(a), east_of(b)) for a in (-1, 1) for b in (-1, 1)]
    )
    for peer in peers:
        pl.semaphore_signal(barrier, inc=1, device_id=peer, device_id_type=MESH)

    r0 = north_ref[0]
    c0 = east_ref[0]
    lane8 = lax.broadcasted_iota(jnp.int32, (SUB, LANES), 1)
    index[0] = jnp.zeros((SUB, LANES), jnp.int32) + r0
    zeros = jnp.zeros((pad, LANES), jnp.float32)
    high[pl.ds(0, pad), :] = zeros
    high[pl.ds(pad + rows, pad), :] = zeros
    own_depth = (
        trigger_ref[0].astype(jnp.float32) * snow_ref[0].astype(jnp.float32) * 0.01
    )
    depth_own[...] = own_depth

    pl.semaphore_wait(barrier, len(peers))

    def remote(src, dst, sends, recvs, slot, peer):
        return pltpu.make_async_remote_copy(
            src_ref=src,
            dst_ref=dst,
            send_sem=sends.at[slot],
            recv_sem=recvs.at[slot],
            device_id=peer,
            device_id_type=MESH,
        )

    index_copies = [
        remote(index.at[0], index.at[d], send_sem, recv_sem, d - 1, (north_of(d), t))
        for d in range(1, groups)
    ]
    for copy in index_copies:
        copy.start()

    load.wait()
    lower = high.at[pl.ds(pad, SUB)]
    upper = high.at[pl.ds(pad + rows - SUB, SUB)]
    halo_copies = []
    for b in (-1, 0, 1):
        halo_copies.append(
            remote(upper, edge_in.at[1 - b], send_sem, recv_sem, groups + 1 - b, (north_of(1), east_of(b)))
        )
        halo_copies.append(
            remote(lower, edge_in.at[4 - b], send_sem, recv_sem, groups + 4 - b, (north_of(-1), east_of(b)))
        )
    base = groups + 6
    halo_copies.append(
        remote(depth_own.at[pl.ds(piece - SUB, SUB)], depth_in.at[0], send_sem, recv_sem, base, (g, east_of(1)))
    )
    halo_copies.append(
        remote(depth_own.at[pl.ds(0, SUB)], depth_in.at[1], send_sem, recv_sem, base + 1, (g, east_of(-1)))
    )
    pack_rows = rows // PACKS
    lane_p = lax.broadcasted_iota(jnp.int32, (pack_rows, LANES), 1)
    step = LANES // PACKS

    strip_copies = []
    for d in range(groups):
        if d > 0:
            index_copies[d - 1].wait_recv()
            first = index[d][0, 0]
        else:
            first = r0
        scenario = north_of(-d)
        start = jnp.clip(first - (REACH + STEPS) - g * rows, -pad, rows) + pad
        part = high[pl.ds(start, span), :]
        if d > 0:
            strip_out[d] = part
            copy = remote(strip_out.at[d], strip_in.at[d], strip_send, strip_recv, d, (scenario, t))
            copy.start()
            strip_copies.append(copy)
        else:
            strip_in[0] = part

    total = jnp.zeros((pack_rows, LANES), jnp.float32)
    for k in range(PACKS):
        part = high[pl.ds(pad + k * pack_rows, pack_rows), :]
        both = jnp.where(lane_p < step // 2, part, pltpu.roll(part, step, 1))
        if k:
            both = pltpu.roll(both, step * k, 1)
        total = jnp.where(lane_p // step == k, both, total)
    packed[...] = total
    halo_copies.append(
        remote(packed, packed_in.at[0], send_sem, recv_sem, base + 2, (g, east_of(1)))
    )
    halo_copies.append(
        remote(packed, packed_in.at[1], send_sem, recv_sem, base + 3, (g, east_of(-1)))
    )
    for copy in halo_copies:
        copy.start()

    for copy in halo_copies:
        copy.wait()

    has_above = g > 0
    has_below = g < groups - 1
    has_left = t > 0
    has_right = t < tiles - 1
    right_half = lane8 < LANES // 2
    for at, slot, here in (
        (pad - SUB, 0, has_above),
        (pad + rows, 3, has_below),
    ):
        high[pl.ds(at, SUB), :] = jnp.where(here, edge_in[slot + 1], 0.0)
        right = jnp.where(jnp.logical_and(here, has_right), edge_in[slot + 2], 0.0)
        left = jnp.where(jnp.logical_and(here, has_left), edge_in[slot], 0.0)
        side[pl.ds(at - pad + 2 * SUB, SUB), :] = jnp.where(right_half, right, left)
    right = jnp.where(has_right, packed_in[1], 0.0)
    left = jnp.where(has_left, packed_in[0], 0.0)
    mixed = jnp.where(lane_p % step < step // 2, right, left)
    for k in range(PACKS):
        ahead = shifted(mixed, step * k, 1)
        behind = shifted(mixed, step * k + step, 1)
        side[pl.ds(2 * SUB + k * pack_rows, pack_rows), :] = jnp.where(
            lane_p < LANES // 2, ahead, behind
        )

    def smooth_rows(at, count):
        def down(ref, offset):
            o = at + offset
            return (
                binomial[0] * (ref[pl.ds(o - 2, count), :] + ref[pl.ds(o + 2, count), :])
                + binomial[1] * (ref[pl.ds(o - 1, count), :] + ref[pl.ds(o + 1, count), :])
                + binomial[2] * ref[pl.ds(o, count), :]
            )

        both = jnp.concatenate([down(high, pad - SUB), down(side, SUB)], axis=1)
        both = (
            binomial[0] * (shifted(both, -2, 1) + shifted(both, 2, 1))
            + binomial[1] * (shifted(both, -1, 1) + shifted(both, 1, 1))
            + binomial[2] * both
        )
        centre = both[:, :LANES]
        right = shifted(both, 1, 1)[:, :LANES]
        left = shifted(both, -1, 1)[:, :LANES]
        smooth[pl.ds(at, count), :] = centre
        diff_c[pl.ds(at, count), :] = right - left
        sum_c[pl.ds(at, count), :] = right + left - 4.0 * centre

    smooth_rows(0, SUB)
    smooth_rows(rows + SUB, SUB)

    def smooth_body(i, carry):
        smooth_rows(pl.multiple_of(SUB + i * CHUNK, SUB), CHUNK)
        return carry

    lax.fori_loop(0, rows // CHUNK, smooth_body, 0)

    for copy in strip_copies:
        copy.wait()
    row_at = lax.broadcasted_iota(jnp.int32, (span, LANES), 0) + (r0 - (REACH + STEPS))
    chosen = strip_in[0]
    for d in range(1, groups):
        source = north_of(d)
        inside = jnp.logical_and(row_at >= source * rows, row_at < source * rows + rows)
        chosen = jnp.where(inside, strip_in[d], chosen)
    strip[...] = chosen
    block_copies = []
    for d in range(1, tiles):
        to = east_of(d)
        copy = remote(
            strip.at[pl.ds(pl.multiple_of(to * piece, SUB), block_rows)],
            block_in.at[t],
            block_send,
            block_recv,
            d,
            (g, to),
        )
        copy.start()
        block_copies.append(copy)
    block_in[t] = strip[pl.ds(pl.multiple_of(t * piece, SUB), block_rows), :]

    def geo_body(i, carry):
        at = pl.multiple_of(i * CHUNK, SUB)
        up = smooth[pl.ds(at + SUB + 1, CHUNK), :]
        low = smooth[pl.ds(at + SUB - 1, CHUNK), :]
        grad_r = (up - low) * 0.25
        grad_c = diff_c[pl.ds(at + SUB, CHUNK), :] * 0.25
        upright = lax.rsqrt(1.0 + grad_r * grad_r + grad_c * grad_c)
        geo[0, pl.ds(at, CHUNK), :] = -grad_r * upright
        geo[1, pl.ds(at, CHUNK), :] = -grad_c * upright
        geo[2, pl.ds(at, CHUNK), :] = upright
        geo[3, pl.ds(at, CHUNK), :] = (up + low + sum_c[pl.ds(at + SUB, CHUNK), :]) * 0.25
        return carry

    lax.fori_loop(0, rows // CHUNK, geo_body, 0)
    store = pltpu.make_async_copy(geo, geo_out, store_sem)
    store.start()

    for copy in block_copies:
        copy.wait()

    first_col = c0 - REACH
    tile_at = lax.shift_right_logical(first_col, 7)
    lane_at = jnp.bitwise_and(first_col, LANES - 1)
    lane_b = lax.broadcasted_iota(jnp.int32, (block_rows, LANES), 1)
    turned = [
        pltpu.roll(block_in[jnp.minimum(tile_at + j, tiles - 1)], LANES - lane_at, 1)
        for j in range(width // LANES + 2)
    ]
    under = jnp.concatenate(
        [
            jnp.where(lane_b < LANES - lane_at, turned[j], turned[j + 1])
            for j in range(width // LANES + 1)
        ],
        axis=1,
    )
    level = five_taps(five_taps(under, 0), 1)
    middle = shifted(level, 1, 0)
    beside = shifted(level, 1, 1)
    patch = normal_fields(
        shifted(beside, 2, 0),
        beside,
        shifted(middle, 2, 1),
        middle,
        shifted(beside, 1, 0),
    )
    patch = tuple(field[:state_rows, :width] for field in patch)

    row = lax.broadcasted_iota(jnp.int32, (state_rows, width), 0) + (t * piece - STEPS)
    col = lax.broadcasted_iota(jnp.int32, (state_rows, width), 1)
    row_ok = jnp.logical_and(row >= 0, row < window_rows)
    depth = jnp.concatenate(
        [depth_in[0][SUB - STEPS :], depth_own[...], depth_in[1][:STEPS]], axis=0
    )
    depth = jnp.where(row_ok, depth, 0.0)
    state[0] = depth
    state[1] = jnp.zeros_like(depth)
    state[2] = jnp.zeros_like(depth)

    def flow_body(i, carry):
        new = flow_step((state[0], state[1], state[2]), patch, row_ok, col)
        for n in range(3):
            state[n] = new[n]
        return carry

    lax.fori_loop(0, STEPS, flow_body, 0)
    for n in range(3):
        flow_out[0, n] = state[n][STEPS : STEPS + piece]

    for copy in index_copies:
        copy.wait_send()
    store.wait()


def shards(height, trigger, snow, north, east):
    groups = lax.axis_size("grp")
    tiles = lax.axis_size("tile")
    rows, cols = height.shape
    _, piece, width = trigger.shape
    block_rows = -(-(piece + 2 * STEPS + 2 * REACH) // SUB) * SUB
    span = piece * (tiles - 1) + block_rows
    state_rows = piece + 2 * STEPS
    f32 = jnp.float32
    pack_rows = rows // PACKS
    vmem = pl.BlockSpec(memory_space=pltpu.VMEM)
    smem = pl.BlockSpec(memory_space=pltpu.SMEM)
    anywhere = pl.BlockSpec(memory_space=pl.ANY)
    dma = pltpu.SemaphoreType.DMA
    small = groups + 10
    return tuple(
        pl.pallas_call(
            functools.partial(kernel, groups, tiles),
            out_shape=(
                jax.ShapeDtypeStruct((4, rows, cols), f32),
                jax.ShapeDtypeStruct((1, 3, piece, width), f32),
            ),
            in_specs=[smem, smem, vmem, vmem, anywhere],
            out_specs=(anywhere, vmem),
            scratch_shapes=[
                pltpu.VMEM((rows + 2 * span, cols), f32),
                pltpu.VMEM((rows + 4 * SUB, LANES), f32),
                pltpu.VMEM((rows + 2 * SUB, LANES), f32),
                pltpu.VMEM((rows + 2 * SUB, LANES), f32),
                pltpu.VMEM((rows + 2 * SUB, LANES), f32),
                pltpu.VMEM((4, rows, cols), f32),
                pltpu.VMEM((pack_rows, LANES), f32),
                pltpu.VMEM((2, pack_rows, LANES), f32),
                pltpu.VMEM((6, SUB, LANES), f32),
                pltpu.VMEM((piece, width), f32),
                pltpu.VMEM((2, SUB, width), f32),
                pltpu.VMEM((groups, SUB, LANES), jnp.int32),
                pltpu.VMEM((groups, span, cols), f32),
                pltpu.VMEM((groups, span, cols), f32),
                pltpu.VMEM((span, cols), f32),
                pltpu.VMEM((tiles, block_rows, cols), f32),
                pltpu.VMEM((3, state_rows, width), f32),
                dma,
                dma,
                dma((small,)),
                dma((small,)),
                dma((groups,)),
                dma((groups,)),
                dma((tiles,)),
                dma((tiles,)),
            ],
            compiler_params=pltpu.CompilerParams(
                collective_id=0, has_side_effects=True, vmem_limit_bytes=48 * 1024 * 1024
            ),
        )(north, east, trigger, snow, height)
    )


def solution(mesh):
    return jax.shard_map(
        shards,
        mesh=mesh,
        in_specs=(
            P("grp", "tile"),
            P("grp", "tile", None),
            P("grp", "tile", None),
            P("grp"),
            P("grp"),
        ),
        out_specs=(P(None, "grp", "tile"), P("grp", None, "tile", None)),
        check_vma=False,
    )
```

```python
import functools
import jax
import jax.numpy as jnp
from jax import lax
from jax.experimental import pallas as pl
from jax.experimental.pallas import tpu as pltpu
from jax.sharding import PartitionSpec as P

STEPS = 4
REACH = 3
LANES = 128
SUB = 8
PACKS = 16
CHUNK = 64
VMEM_MIB = 60

cell_size = 2.0
gravity = 9.81
time_step = 0.1
friction = 0.2
turbulence = 500.0
depth_floor = 0.1
speed_floor = 0.5
binomial = (0.0625, 0.25, 0.375, 0.25, 0.0625)
still_wave = (gravity * depth_floor) ** 0.5

MESH = pl.DeviceIdType.MESH


def shifted(x, by, axis):
    size = x.shape[axis]
    by = by % size
    return x if by == 0 else pltpu.roll(x, size - by, axis)


def five_taps(x, axis):
    outer = x + shifted(x, 4, axis)
    inner = shifted(x, 1, axis) + shifted(x, 3, axis)
    return binomial[0] * outer + binomial[1] * inner + binomial[2] * shifted(x, 2, axis)


def normal_fields(up, low, right, left, centre):
    grad_r = (up - low) * 0.25
    grad_c = (right - left) * 0.25
    curvature = (up + low + right + left - 4.0 * centre) * 0.25
    upright = lax.rsqrt(1.0 + grad_r * grad_r + grad_c * grad_c)
    return -grad_r * upright, -grad_c * upright, upright, curvature


def flow_step(state, patch, row_ok, col):
    depth, mom_r, mom_c = state
    n_r, n_c, n_z, kappa = patch
    width = depth.shape[1]
    inv = 1.0 / jnp.maximum(depth, depth_floor)
    u_r = mom_r * inv
    u_c = mom_c * inv
    wave = jnp.sqrt(gravity * (jnp.maximum(depth, 0.0) + depth_floor))
    pressure = 0.5 * gravity * depth * depth

    reach = jnp.abs(u_r) + wave
    bound = jnp.maximum(reach, shifted(reach, 1, 0))
    gains = []
    for q, f in (
        (depth, mom_r),
        (mom_r, mom_r * u_r + pressure),
        (mom_c, mom_c * u_r),
    ):
        face = (f + shifted(f, 1, 0)) - bound * (shifted(q, 1, 0) - q)
        gains.append(face - shifted(face, -1, 0))

    reach = jnp.abs(u_c) + wave
    last = col == width - 1
    first = col == 0
    bound = jnp.maximum(reach, jnp.where(last, still_wave, shifted(reach, 1, 1)))
    rim_bound = jnp.maximum(reach, still_wave)
    totals = []
    for gain, q, f in zip(
        gains,
        (depth, mom_r, mom_c),
        (mom_c, mom_r * u_c, mom_c * u_c + pressure),
    ):
        q_next = jnp.where(last, 0.0, shifted(q, 1, 1))
        f_next = jnp.where(last, 0.0, shifted(f, 1, 1))
        face = (f + f_next) - bound * (q_next - q)
        before = jnp.where(first, f - rim_bound * q, shifted(face, -1, 1))
        totals.append(gain + (face - before))

    scale = 0.5 * time_step / cell_size
    new_depth = depth - scale * totals[0]
    push = time_step * gravity * depth
    new_r = mom_r - scale * totals[1] + push * n_r
    new_c = mom_c - scale * totals[2] + push * n_c
    inv = 1.0 / jnp.maximum(new_depth, depth_floor)
    v_r = new_r * inv
    v_c = new_c * inv
    square = v_r * v_r + v_c * v_c
    energy = square + speed_floor * speed_floor
    inv_speed = lax.rsqrt(energy)
    load = jnp.maximum(gravity * n_z + kappa * square, 0.0)
    drag = time_step * (
        friction * load * inv_speed + (gravity / turbulence) * (energy * inv_speed) * inv
    )
    damp = 1.0 / (1.0 + drag)
    return (
        jnp.where(row_ok, new_depth, 0.0),
        jnp.where(row_ok, new_r * damp, 0.0),
        jnp.where(row_ok, new_c * damp, 0.0),
    )


def exchange(
    groups,
    tiles,
    north_hbm,
    trigger_hbm,
    snow_hbm,
    height_hbm,
    geo_out,
    block_out,
    depth_out,
    high,
    side,
    smooth,
    diff_c,
    sum_c,
    geo,
    packed,
    packed_in,
    edge_in,
    depth_own,
    depth_in,
    depth_all,
    index,
    strip_out,
    strip_in,
    strip,
    north_ref,
    trigger_ref,
    snow_ref,
    load_sem,
    store_sem,
    send_sem,
    recv_sem,
    strip_send,
    strip_recv,
    block_send,
    block_recv,
):
    g = lax.axis_index("grp")
    t = lax.axis_index("tile")
    rows = height_hbm.shape[0]
    piece = trigger_hbm.shape[1]
    width = trigger_hbm.shape[2]
    span = strip.shape[0]
    block_rows = block_out.shape[1]
    window_rows = piece * tiles
    pad = span
    state_rows = piece + 2 * STEPS
    north_of = lambda d: lax.rem(g + d + groups, groups)
    east_of = lambda d: lax.rem(t + d + tiles, tiles)
    other = g + 1 - 2 * lax.rem(g, 2)
    across = lax.rem(g + 2, groups)
    across_other = lax.rem(other + 2, groups)

    loads = [
        pltpu.make_async_copy(source, target, load_sem.at[n])
        for n, (source, target) in enumerate(
            (
                (north_hbm, north_ref),
                (height_hbm, high.at[pl.ds(pad, rows)]),
                (trigger_hbm, trigger_ref),
                (snow_hbm, snow_ref),
            )
        )
    ]
    for load in loads:
        load.start()

    barrier = pltpu.get_barrier_semaphore()
    peers = (
        [(other, t), (across, t), (across_other, t)]
        + [(g, east_of(d)) for d in range(1, tiles)]
        + [(north_of(a), east_of(b)) for a in (-1, 1) for b in (-1, 1)]
    )
    for peer in peers:
        pl.semaphore_signal(barrier, inc=1, device_id=peer, device_id_type=MESH)

    lane8 = lax.broadcasted_iota(jnp.int32, (SUB, LANES), 1)
    loads[0].wait()
    r0 = north_ref[0]
    index[0] = jnp.zeros((SUB, LANES), jnp.int32) + r0
    zeros = jnp.zeros((pad, LANES), jnp.float32)
    high[pl.ds(0, pad), :] = zeros
    high[pl.ds(pad + rows, pad), :] = zeros
    loads[2].wait()
    loads[3].wait()
    own_depth = (
        trigger_ref[0].astype(jnp.float32) * snow_ref[0].astype(jnp.float32) * 0.01
    )
    depth_own[...] = own_depth

    loads[1].wait()
    pack_rows = rows // PACKS
    lane_p = lax.broadcasted_iota(jnp.int32, (pack_rows, LANES), 1)
    step = LANES // PACKS
    total = jnp.zeros((pack_rows, LANES), jnp.float32)
    for k in range(PACKS):
        part = high[pl.ds(pad + k * pack_rows, pack_rows), :]
        both = jnp.where(lane_p < step // 2, part, pltpu.roll(part, step, 1))
        if k:
            both = pltpu.roll(both, step * k, 1)
        total = jnp.where(lane_p // step == k, both, total)
    packed[...] = total

    pl.semaphore_wait(barrier, len(peers))

    def remote(src, dst, sends, recvs, slot, peer):
        return pltpu.make_async_remote_copy(
            src_ref=src,
            dst_ref=dst,
            send_sem=sends.at[slot],
            recv_sem=recvs.at[slot],
            device_id=peer,
            device_id_type=MESH,
        )

    index_copies = [
        remote(index.at[0], index.at[d], send_sem, recv_sem, d - 1, (peer, t))
        for d, peer in ((3, across_other), (2, across), (1, other))
    ]
    lower = high.at[pl.ds(pad, SUB)]
    upper = high.at[pl.ds(pad + rows - SUB, SUB)]
    base = groups + 6
    halo_copies = [
        remote(packed, packed_in.at[0], send_sem, recv_sem, base + 2, (g, east_of(1))),
        remote(packed, packed_in.at[1], send_sem, recv_sem, base + 3, (g, east_of(-1))),
    ]
    for b in (-1, 0, 1):
        halo_copies.append(
            remote(upper, edge_in.at[1 - b], send_sem, recv_sem, groups + 1 - b, (north_of(1), east_of(b)))
        )
        halo_copies.append(
            remote(lower, edge_in.at[4 - b], send_sem, recv_sem, groups + 4 - b, (north_of(-1), east_of(b)))
        )
    depth_copies = [
        remote(depth_own.at[pl.ds(piece - SUB, SUB)], depth_in.at[0], send_sem, recv_sem, base, (g, east_of(1))),
        remote(depth_own.at[pl.ds(0, SUB)], depth_in.at[1], send_sem, recv_sem, base + 1, (g, east_of(-1))),
    ]
    for copy in index_copies + halo_copies + depth_copies:
        copy.start()

    def part_of(first):
        start = jnp.clip(first - (REACH + STEPS) - g * rows, -pad, rows) + pad
        return high[pl.ds(start, span), :]

    index_copies[0].wait_recv()
    strip_out[0] = part_of(index[3][0, 0])
    far = remote(strip_out.at[0], strip_in.at[0], strip_send, strip_recv, 0, (other, t))
    far.start()
    index_copies[2].wait_recv()
    strip_out[1] = part_of(index[1][0, 0])
    near = remote(strip_out.at[1], strip_in.at[1], strip_send, strip_recv, 1, (other, t))
    near.start()
    index_copies[1].wait_recv()
    first_across = index[2][0, 0]
    strip_out[2] = part_of(first_across)
    strip[...] = part_of(r0)

    row_in = lax.broadcasted_iota(jnp.int32, (span, LANES), 0) - (REACH + STEPS)

    def of_block(first, block):
        return jnp.logical_and(row_in >= block * rows - first, row_in < (block + 1) * rows - first)

    far.wait()
    strip_out[2] = jnp.where(of_block(first_across, other), strip_in[0], strip_out[2])
    long = remote(strip_out.at[2], strip_in.at[2], strip_send, strip_recv, 2, (across, t))
    long.start()

    for copy in halo_copies:
        copy.wait()

    has_above = g > 0
    has_below = g < groups - 1
    has_left = t > 0
    has_right = t < tiles - 1
    right_half = lane8 < LANES // 2
    for at, slot, here in (
        (pad - SUB, 0, has_above),
        (pad + rows, 3, has_below),
    ):
        high[pl.ds(at, SUB), :] = jnp.where(here, edge_in[slot + 1], 0.0)
        right = jnp.where(jnp.logical_and(here, has_right), edge_in[slot + 2], 0.0)
        left = jnp.where(jnp.logical_and(here, has_left), edge_in[slot], 0.0)
        side[pl.ds(at - pad + 2 * SUB, SUB), :] = jnp.where(right_half, right, left)
    side[pl.ds(0, SUB), :] = jnp.zeros((SUB, LANES), jnp.float32)
    side[pl.ds(rows + 3 * SUB, SUB), :] = jnp.zeros((SUB, LANES), jnp.float32)
    right = jnp.where(has_right, packed_in[1], 0.0)
    left = jnp.where(has_left, packed_in[0], 0.0)
    mixed = jnp.where(lane_p % step < step // 2, right, left)
    for k in range(PACKS):
        ahead = shifted(mixed, step * k, 1)
        behind = shifted(mixed, step * k + step, 1)
        side[pl.ds(2 * SUB + k * pack_rows, pack_rows), :] = jnp.where(
            lane_p < LANES // 2, ahead, behind
        )

    def smooth_rows(at, count):
        def down(ref, offset):
            o = at + offset
            return (
                binomial[0] * (ref[pl.ds(o - 2, count), :] + ref[pl.ds(o + 2, count), :])
                + binomial[1] * (ref[pl.ds(o - 1, count), :] + ref[pl.ds(o + 1, count), :])
                + binomial[2] * ref[pl.ds(o, count), :]
            )

        both = jnp.concatenate([down(high, pad - SUB), down(side, SUB)], axis=1)
        both = (
            binomial[0] * (shifted(both, -2, 1) + shifted(both, 2, 1))
            + binomial[1] * (shifted(both, -1, 1) + shifted(both, 1, 1))
            + binomial[2] * both
        )
        centre = both[:, :LANES]
        right = shifted(both, 1, 1)[:, :LANES]
        left = shifted(both, -1, 1)[:, :LANES]
        smooth[pl.ds(at, count), :] = centre
        diff_c[pl.ds(at, count), :] = right - left
        sum_c[pl.ds(at, count), :] = right + left - 4.0 * centre

    smooth_rows(0, SUB)
    smooth_rows(rows + SUB, SUB)

    def smooth_body(i, carry):
        smooth_rows(pl.multiple_of(SUB + i * CHUNK, SUB), CHUNK)
        return carry

    lax.fori_loop(0, rows // CHUNK, smooth_body, 0)

    near.wait()
    long.wait()
    strip[...] = jnp.where(
        of_block(r0, g),
        strip[...],
        jnp.where(of_block(r0, other), strip_in[1], strip_in[2]),
    )
    block_copies = []
    for d in range(1, tiles):
        to = east_of(d)
        copy = remote(
            strip.at[pl.ds(pl.multiple_of(to * piece, SUB), block_rows)],
            block_out.at[t],
            block_send,
            block_recv,
            d,
            (g, to),
        )
        copy.start()
        block_copies.append(copy)
    stores = [
        pltpu.make_async_copy(
            strip.at[pl.ds(pl.multiple_of(t * piece, SUB), block_rows)],
            block_out.at[t],
            store_sem.at[0],
        )
    ]
    stores[0].start()

    for copy in depth_copies:
        copy.wait()
    row = lax.broadcasted_iota(jnp.int32, (state_rows, width), 0) + (t * piece - STEPS)
    row_ok = jnp.logical_and(row >= 0, row < window_rows)
    depth = jnp.concatenate(
        [depth_in[0][SUB - STEPS :], depth_own[...], depth_in[1][:STEPS]], axis=0
    )
    depth_all[...] = jnp.where(row_ok, depth, 0.0)
    stores.append(pltpu.make_async_copy(depth_all, depth_out, store_sem.at[1]))
    stores[1].start()

    def geo_body(i, carry):
        at = pl.multiple_of(i * CHUNK, SUB)
        up = smooth[pl.ds(at + SUB + 1, CHUNK), :]
        low = smooth[pl.ds(at + SUB - 1, CHUNK), :]
        grad_r = (up - low) * 0.25
        grad_c = diff_c[pl.ds(at + SUB, CHUNK), :] * 0.25
        upright = lax.rsqrt(1.0 + grad_r * grad_r + grad_c * grad_c)
        geo[0, pl.ds(at, CHUNK), :] = -grad_r * upright
        geo[1, pl.ds(at, CHUNK), :] = -grad_c * upright
        geo[2, pl.ds(at, CHUNK), :] = upright
        geo[3, pl.ds(at, CHUNK), :] = (up + low + sum_c[pl.ds(at + SUB, CHUNK), :]) * 0.25
        return carry

    lax.fori_loop(0, rows // CHUNK, geo_body, 0)
    stores.append(pltpu.make_async_copy(geo, geo_out, store_sem.at[2]))
    stores[2].start()

    for copy in block_copies:
        copy.wait()
    for copy in index_copies:
        copy.wait_send()
    for store in stores:
        store.wait()


def flow(
    tiles,
    east_hbm,
    geo_in,
    block_hbm,
    depth_hbm,
    geo_out,
    flow_out,
    east_ref,
    block_in,
    state,
    result,
    geo_held,
    load_sem,
    geo_sem,
    store_sem,
):
    t = lax.axis_index("tile")
    state_rows, width = depth_hbm.shape
    piece = state_rows - 2 * STEPS
    block_rows = block_in.shape[1]
    loads = [
        pltpu.make_async_copy(source, target, load_sem.at[n])
        for n, (source, target) in enumerate(
            ((east_hbm, east_ref), (block_hbm, block_in), (depth_hbm, state.at[0]))
        )
    ]
    for load in loads:
        load.start()
    geo_loads = [
        pltpu.make_async_copy(geo_in.at[n], geo_held.at[n], geo_sem.at[n]) for n in range(4)
    ]
    for load in geo_loads:
        load.start()
    for load in loads:
        load.wait()

    first_col = east_ref[0] - REACH
    tile_at = lax.shift_right_logical(first_col, 7)
    lane_at = jnp.bitwise_and(first_col, LANES - 1)
    lane_b = lax.broadcasted_iota(jnp.int32, (block_rows, LANES), 1)
    turned = [
        pltpu.roll(block_in[jnp.minimum(tile_at + j, tiles - 1)], LANES - lane_at, 1)
        for j in range(width // LANES + 2)
    ]
    under = jnp.concatenate(
        [
            jnp.where(lane_b < LANES - lane_at, turned[j], turned[j + 1])
            for j in range(width // LANES + 1)
        ],
        axis=1,
    )
    level = five_taps(five_taps(under, 0), 1)
    middle = shifted(level, 1, 0)
    beside = shifted(level, 1, 1)
    patch = normal_fields(
        shifted(beside, 2, 0),
        beside,
        shifted(middle, 2, 1),
        middle,
        shifted(beside, 1, 0),
    )
    patch = tuple(field[:state_rows, :width] for field in patch)
    geo_stores = []
    for n in range(4):
        geo_loads[n].wait()
        geo_stores.append(pltpu.make_async_copy(geo_held.at[n], geo_out.at[n], geo_sem.at[4 + n]))
        geo_stores[n].start()

    row = lax.broadcasted_iota(jnp.int32, (state_rows, width), 0) + (t * piece - STEPS)
    col = lax.broadcasted_iota(jnp.int32, (state_rows, width), 1)
    row_ok = jnp.logical_and(row >= 0, row < piece * tiles)
    state[1] = jnp.zeros((state_rows, width), jnp.float32)
    state[2] = jnp.zeros((state_rows, width), jnp.float32)

    def flow_body(i, carry):
        new = flow_step((state[0], state[1], state[2]), patch, row_ok, col)
        for n in range(3):
            state[n] = new[n]
        return carry

    lax.fori_loop(0, STEPS, flow_body, 0)
    for n in range(3):
        result[0, n] = state[n][STEPS : STEPS + piece]
    store = pltpu.make_async_copy(result, flow_out, store_sem)
    store.start()
    store.wait()
    for copy in geo_stores:
        copy.wait()


def shards(height, trigger, snow, north, east):
    groups = lax.axis_size("grp")
    tiles = lax.axis_size("tile")
    rows, cols = height.shape
    _, piece, width = trigger.shape
    assert groups == 4 and cols == LANES and rows % (PACKS * SUB) == 0 and rows % CHUNK == 0
    block_rows = -(-(piece + 2 * STEPS + 2 * REACH) // SUB) * SUB
    span = piece * (tiles - 1) + block_rows
    state_rows = piece + 2 * STEPS
    f32 = jnp.float32
    pack_rows = rows // PACKS
    anywhere = pl.BlockSpec(memory_space=pl.ANY)
    dma = pltpu.SemaphoreType.DMA
    small = groups + 10
    mib = 1024 * 1024
    geo, blocks, depth = pl.pallas_call(
        functools.partial(exchange, groups, tiles),
        out_shape=(
            jax.ShapeDtypeStruct((4, rows, cols), f32),
            jax.ShapeDtypeStruct((tiles, block_rows, cols), f32),
            jax.ShapeDtypeStruct((state_rows, width), f32),
        ),
        in_specs=[anywhere] * 4,
        out_specs=(anywhere,) * 3,
        scratch_shapes=[
            pltpu.VMEM((rows + 2 * span, cols), f32),
            pltpu.VMEM((rows + 4 * SUB, LANES), f32),
            pltpu.VMEM((rows + 2 * SUB, LANES), f32),
            pltpu.VMEM((rows + 2 * SUB, LANES), f32),
            pltpu.VMEM((rows + 2 * SUB, LANES), f32),
            pltpu.VMEM((4, rows, cols), f32),
            pltpu.VMEM((pack_rows, LANES), f32),
            pltpu.VMEM((2, pack_rows, LANES), f32),
            pltpu.VMEM((6, SUB, LANES), f32),
            pltpu.VMEM((piece, width), f32),
            pltpu.VMEM((2, SUB, width), f32),
            pltpu.VMEM((state_rows, width), f32),
            pltpu.VMEM((groups, SUB, LANES), jnp.int32),
            pltpu.VMEM((3, span, cols), f32),
            pltpu.VMEM((3, span, cols), f32),
            pltpu.VMEM((span, cols), f32),
            pltpu.SMEM((1,), jnp.int32),
            pltpu.VMEM((1, piece, width), jnp.int32),
            pltpu.VMEM((1, piece, width), jnp.int32),
            dma((4,)),
            dma((3,)),
            dma((small,)),
            dma((small,)),
            dma((3,)),
            dma((3,)),
            dma((tiles,)),
            dma((tiles,)),
        ],
        compiler_params=pltpu.CompilerParams(
            collective_id=0, has_side_effects=True, vmem_limit_bytes=VMEM_MIB * mib
        ),
    )(north, trigger, snow, height)
    return tuple(
        pl.pallas_call(
            functools.partial(flow, tiles),
            out_shape=(
                jax.ShapeDtypeStruct((4, rows, cols), f32),
                jax.ShapeDtypeStruct((1, 3, piece, width), f32),
            ),
            in_specs=[anywhere] * 4,
            out_specs=(anywhere,) * 2,
            scratch_shapes=[
                pltpu.SMEM((1,), jnp.int32),
                pltpu.VMEM((tiles, block_rows, cols), f32),
                pltpu.VMEM((3, state_rows, width), f32),
                pltpu.VMEM((1, 3, piece, width), f32),
                pltpu.VMEM((4, rows, cols), f32),
                dma((3,)),
                dma((8,)),
                dma,
            ],
            compiler_params=pltpu.CompilerParams(vmem_limit_bytes=VMEM_MIB * mib),
        )(east, geo, blocks, depth)
    )


def solution(mesh):
    return jax.shard_map(
        shards,
        mesh=mesh,
        in_specs=(
            P("grp", "tile"),
            P("grp", "tile", None),
            P("grp", "tile", None),
            P("grp"),
            P("grp"),
        ),
        out_specs=(P(None, "grp", "tile"), P("grp", None, "tile", None)),
        check_vma=False,
    )
```

```python
import functools
import jax
import jax.numpy as jnp
from jax import lax
from jax.experimental import pallas as pl
from jax.experimental.pallas import tpu as pltpu
from jax.sharding import PartitionSpec as P

STEPS = 4
REACH = 3
LANES = 128
SUB = 8
PACKS = 16
CHUNK = 64
VMEM_MIB = 60

cell_size = 2.0
gravity = 9.81
time_step = 0.1
friction = 0.2
turbulence = 500.0
depth_floor = 0.1
speed_floor = 0.5
binomial = (0.0625, 0.25, 0.375, 0.25, 0.0625)
still_wave = (gravity * depth_floor) ** 0.5

MESH = pl.DeviceIdType.MESH


def shifted(x, by, axis):
    size = x.shape[axis]
    by = by % size
    return x if by == 0 else pltpu.roll(x, size - by, axis)


def five_taps(x, axis):
    outer = x + shifted(x, 4, axis)
    inner = shifted(x, 1, axis) + shifted(x, 3, axis)
    return binomial[0] * outer + binomial[1] * inner + binomial[2] * shifted(x, 2, axis)


def normal_fields(up, low, right, left, centre):
    grad_r = (up - low) * 0.25
    grad_c = (right - left) * 0.25
    curvature = (up + low + right + left - 4.0 * centre) * 0.25
    upright = lax.rsqrt(1.0 + grad_r * grad_r + grad_c * grad_c)
    return -grad_r * upright, -grad_c * upright, upright, curvature


def flow_step(state, patch, row_ok, col):
    depth, mom_r, mom_c = state
    width = depth.shape[1]
    inv = 1.0 / jnp.maximum(depth, depth_floor)
    u_r = mom_r * inv
    u_c = mom_c * inv
    wave = jnp.sqrt(gravity * (jnp.maximum(depth, 0.0) + depth_floor))
    pressure = 0.5 * gravity * depth * depth

    reach = jnp.abs(u_r) + wave
    bound = jnp.maximum(reach, shifted(reach, 1, 0))
    gains = []
    for q, f in (
        (depth, mom_r),
        (mom_r, mom_r * u_r + pressure),
        (mom_c, mom_c * u_r),
    ):
        face = (f + shifted(f, 1, 0)) - bound * (shifted(q, 1, 0) - q)
        gains.append(face - shifted(face, -1, 0))

    reach = jnp.abs(u_c) + wave
    last = col == width - 1
    first = col == 0
    bound = jnp.maximum(reach, jnp.where(last, still_wave, shifted(reach, 1, 1)))
    rim_bound = jnp.maximum(reach, still_wave)
    totals = []
    for gain, q, f in zip(
        gains,
        (depth, mom_r, mom_c),
        (mom_c, mom_r * u_c, mom_c * u_c + pressure),
    ):
        q_next = jnp.where(last, 0.0, shifted(q, 1, 1))
        f_next = jnp.where(last, 0.0, shifted(f, 1, 1))
        face = (f + f_next) - bound * (q_next - q)
        before = jnp.where(first, f - rim_bound * q, shifted(face, -1, 1))
        totals.append(gain + (face - before))

    return finish_step(depth, mom_r, mom_c, totals, patch, row_ok)


def finish_step(depth, mom_r, mom_c, totals, patch, row_ok):
    n_r, n_c, n_z, kappa = patch
    scale = 0.5 * time_step / cell_size
    new_depth = depth - scale * totals[0]
    push = time_step * gravity * depth
    new_r = mom_r - scale * totals[1] + push * n_r
    new_c = mom_c - scale * totals[2] + push * n_c
    inv = 1.0 / jnp.maximum(new_depth, depth_floor)
    v_r = new_r * inv
    v_c = new_c * inv
    square = v_r * v_r + v_c * v_c
    energy = square + speed_floor * speed_floor
    inv_speed = lax.rsqrt(energy)
    load = jnp.maximum(gravity * n_z + kappa * square, 0.0)
    drag = time_step * (
        friction * load * inv_speed + (gravity / turbulence) * (energy * inv_speed) * inv
    )
    damp = 1.0 / (1.0 + drag)
    return (
        jnp.where(row_ok, new_depth, 0.0),
        jnp.where(row_ok, new_r * damp, 0.0),
        jnp.where(row_ok, new_c * damp, 0.0),
    )


def first_flow_step(depth, patch, row_ok, col):
    width = depth.shape[1]
    wave = jnp.sqrt(gravity * (jnp.maximum(depth, 0.0) + depth_floor))
    pressure = 0.5 * gravity * depth * depth

    bound = jnp.maximum(wave, shifted(wave, 1, 0))
    face = bound * (depth - shifted(depth, 1, 0))
    gain = face - shifted(face, -1, 0)
    gain_r = shifted(pressure, 1, 0) - shifted(pressure, -1, 0)

    last = col == width - 1
    first = col == 0
    bound = jnp.maximum(wave, jnp.where(last, still_wave, shifted(wave, 1, 1)))
    face = bound * (depth - jnp.where(last, 0.0, shifted(depth, 1, 1)))
    before = jnp.where(first, -jnp.maximum(wave, still_wave) * depth, shifted(face, -1, 1))
    gain = gain + (face - before)
    gain_c = jnp.where(last, 0.0, shifted(pressure, 1, 1)) - jnp.where(
        first, 0.0, shifted(pressure, -1, 1)
    )
    return finish_step(depth, 0.0, 0.0, (gain, gain_r, gain_c), patch, row_ok)


def exchange(
    groups,
    tiles,
    north_hbm,
    trigger_hbm,
    snow_hbm,
    height_hbm,
    geo_out,
    block_out,
    depth_out,
    high,
    side,
    smooth,
    diff_c,
    sum_c,
    geo,
    packed,
    packed_in,
    edge_in,
    depth_own,
    depth_in,
    depth_all,
    index,
    strip_out,
    strip_in,
    strip,
    north_ref,
    trigger_ref,
    snow_ref,
    load_sem,
    store_sem,
    send_sem,
    recv_sem,
    strip_send,
    strip_recv,
    block_send,
    block_recv,
):
    g = lax.axis_index("grp")
    t = lax.axis_index("tile")
    rows = height_hbm.shape[0]
    piece = trigger_hbm.shape[1]
    width = trigger_hbm.shape[2]
    span = strip.shape[0]
    block_rows = block_out.shape[1]
    window_rows = piece * tiles
    pad = span
    state_rows = piece + 2 * STEPS
    north_of = lambda d: lax.rem(g + d + groups, groups)
    east_of = lambda d: lax.rem(t + d + tiles, tiles)
    other = g + 1 - 2 * lax.rem(g, 2)
    across = lax.rem(g + 2, groups)
    across_other = lax.rem(other + 2, groups)

    loads = [
        pltpu.make_async_copy(source, target, load_sem.at[n])
        for n, (source, target) in enumerate(
            (
                (north_hbm, north_ref),
                (height_hbm, high.at[pl.ds(pad, rows)]),
                (trigger_hbm, trigger_ref),
                (snow_hbm, snow_ref),
            )
        )
    ]
    for load in loads:
        load.start()

    barrier = pltpu.get_barrier_semaphore()
    peers = (
        [(other, t), (across, t), (across_other, t)]
        + [(g, east_of(d)) for d in range(1, tiles)]
        + [(north_of(a), east_of(b)) for a in (-1, 1) for b in (-1, 1)]
    )
    for peer in peers:
        pl.semaphore_signal(barrier, inc=1, device_id=peer, device_id_type=MESH)

    lane8 = lax.broadcasted_iota(jnp.int32, (SUB, LANES), 1)
    loads[0].wait()
    r0 = north_ref[0]
    index[0] = jnp.zeros((SUB, LANES), jnp.int32) + r0
    zeros = jnp.zeros((pad, LANES), jnp.float32)
    high[pl.ds(0, pad), :] = zeros
    high[pl.ds(pad + rows, pad), :] = zeros
    loads[2].wait()
    loads[3].wait()
    own_depth = (
        trigger_ref[0].astype(jnp.float32) * snow_ref[0].astype(jnp.float32) * 0.01
    )
    depth_own[...] = own_depth

    loads[1].wait()
    pack_rows = rows // PACKS
    lane_p = lax.broadcasted_iota(jnp.int32, (pack_rows, LANES), 1)
    step = LANES // PACKS
    total = jnp.zeros((pack_rows, LANES), jnp.float32)
    for k in range(PACKS):
        part = high[pl.ds(pad + k * pack_rows, pack_rows), :]
        both = jnp.where(lane_p < step // 2, part, pltpu.roll(part, step, 1))
        if k:
            both = pltpu.roll(both, step * k, 1)
        total = jnp.where(lane_p // step == k, both, total)
    packed[...] = total

    pl.semaphore_wait(barrier, len(peers))

    def remote(src, dst, sends, recvs, slot, peer):
        return pltpu.make_async_remote_copy(
            src_ref=src,
            dst_ref=dst,
            send_sem=sends.at[slot],
            recv_sem=recvs.at[slot],
            device_id=peer,
            device_id_type=MESH,
        )

    index_copies = [
        remote(index.at[0], index.at[d], send_sem, recv_sem, d - 1, (peer, t))
        for d, peer in ((3, across_other), (2, across), (1, other))
    ]
    lower = high.at[pl.ds(pad, SUB)]
    upper = high.at[pl.ds(pad + rows - SUB, SUB)]
    base = groups + 6
    halo_copies = [
        remote(packed, packed_in.at[0], send_sem, recv_sem, base + 2, (g, east_of(1))),
        remote(packed, packed_in.at[1], send_sem, recv_sem, base + 3, (g, east_of(-1))),
    ]
    for b in (-1, 0, 1):
        halo_copies.append(
            remote(upper, edge_in.at[1 - b], send_sem, recv_sem, groups + 1 - b, (north_of(1), east_of(b)))
        )
        halo_copies.append(
            remote(lower, edge_in.at[4 - b], send_sem, recv_sem, groups + 4 - b, (north_of(-1), east_of(b)))
        )
    depth_copies = [
        remote(depth_own.at[pl.ds(piece - SUB, SUB)], depth_in.at[0], send_sem, recv_sem, base, (g, east_of(1))),
        remote(depth_own.at[pl.ds(0, SUB)], depth_in.at[1], send_sem, recv_sem, base + 1, (g, east_of(-1))),
    ]
    for copy in index_copies + halo_copies + depth_copies:
        copy.start()

    def part_of(first):
        start = jnp.clip(first - (REACH + STEPS) - g * rows, -pad, rows) + pad
        return high[pl.ds(start, span), :]

    index_copies[0].wait_recv()
    strip_out[0] = part_of(index[3][0, 0])
    far = remote(strip_out.at[0], strip_in.at[0], strip_send, strip_recv, 0, (other, t))
    far.start()
    index_copies[2].wait_recv()
    strip_out[1] = part_of(index[1][0, 0])
    near = remote(strip_out.at[1], strip_in.at[1], strip_send, strip_recv, 1, (other, t))
    near.start()
    index_copies[1].wait_recv()
    first_across = index[2][0, 0]
    strip_out[2] = part_of(first_across)
    strip[...] = part_of(r0)

    row_in = lax.broadcasted_iota(jnp.int32, (span, LANES), 0) - (REACH + STEPS)

    def of_block(first, block):
        return jnp.logical_and(row_in >= block * rows - first, row_in < (block + 1) * rows - first)

    far.wait()
    strip_out[2] = jnp.where(of_block(first_across, other), strip_in[0], strip_out[2])
    long = remote(strip_out.at[2], strip_in.at[2], strip_send, strip_recv, 2, (across, t))
    long.start()

    for copy in halo_copies:
        copy.wait()

    has_above = g > 0
    has_below = g < groups - 1
    has_left = t > 0
    has_right = t < tiles - 1
    right_half = lane8 < LANES // 2
    for at, slot, here in (
        (pad - SUB, 0, has_above),
        (pad + rows, 3, has_below),
    ):
        high[pl.ds(at, SUB), :] = jnp.where(here, edge_in[slot + 1], 0.0)
        right = jnp.where(jnp.logical_and(here, has_right), edge_in[slot + 2], 0.0)
        left = jnp.where(jnp.logical_and(here, has_left), edge_in[slot], 0.0)
        side[pl.ds(at - pad + 2 * SUB, SUB), :] = jnp.where(right_half, right, left)
    side[pl.ds(0, SUB), :] = jnp.zeros((SUB, LANES), jnp.float32)
    side[pl.ds(rows + 3 * SUB, SUB), :] = jnp.zeros((SUB, LANES), jnp.float32)
    right = jnp.where(has_right, packed_in[1], 0.0)
    left = jnp.where(has_left, packed_in[0], 0.0)
    mixed = jnp.where(lane_p % step < step // 2, right, left)
    for k in range(PACKS):
        ahead = shifted(mixed, step * k, 1)
        behind = shifted(mixed, step * k + step, 1)
        side[pl.ds(2 * SUB + k * pack_rows, pack_rows), :] = jnp.where(
            lane_p < LANES // 2, ahead, behind
        )

    def smooth_rows(at, count):
        def down(ref, offset):
            o = at + offset
            return (
                binomial[0] * (ref[pl.ds(o - 2, count), :] + ref[pl.ds(o + 2, count), :])
                + binomial[1] * (ref[pl.ds(o - 1, count), :] + ref[pl.ds(o + 1, count), :])
                + binomial[2] * ref[pl.ds(o, count), :]
            )

        both = jnp.concatenate([down(high, pad - SUB), down(side, SUB)], axis=1)
        both = (
            binomial[0] * (shifted(both, -2, 1) + shifted(both, 2, 1))
            + binomial[1] * (shifted(both, -1, 1) + shifted(both, 1, 1))
            + binomial[2] * both
        )
        centre = both[:, :LANES]
        right = shifted(both, 1, 1)[:, :LANES]
        left = shifted(both, -1, 1)[:, :LANES]
        smooth[pl.ds(at, count), :] = centre
        diff_c[pl.ds(at, count), :] = right - left
        sum_c[pl.ds(at, count), :] = right + left - 4.0 * centre

    smooth_rows(0, SUB)
    smooth_rows(rows + SUB, SUB)

    def smooth_body(i, carry):
        smooth_rows(pl.multiple_of(SUB + i * CHUNK, SUB), CHUNK)
        return carry

    lax.fori_loop(0, rows // CHUNK, smooth_body, 0)

    near.wait()
    long.wait()
    strip[...] = jnp.where(
        of_block(r0, g),
        strip[...],
        jnp.where(of_block(r0, other), strip_in[1], strip_in[2]),
    )
    block_copies = []
    for d in range(1, tiles):
        to = east_of(d)
        copy = remote(
            strip.at[pl.ds(pl.multiple_of(to * piece, SUB), block_rows)],
            block_out.at[t],
            block_send,
            block_recv,
            d,
            (g, to),
        )
        copy.start()
        block_copies.append(copy)
    stores = [
        pltpu.make_async_copy(
            strip.at[pl.ds(pl.multiple_of(t * piece, SUB), block_rows)],
            block_out.at[t],
            store_sem.at[0],
        )
    ]
    stores[0].start()

    for copy in depth_copies:
        copy.wait()
    row = lax.broadcasted_iota(jnp.int32, (state_rows, width), 0) + (t * piece - STEPS)
    row_ok = jnp.logical_and(row >= 0, row < window_rows)
    depth = jnp.concatenate(
        [depth_in[0][SUB - STEPS :], depth_own[...], depth_in[1][:STEPS]], axis=0
    )
    depth_all[...] = jnp.where(row_ok, depth, 0.0)
    stores.append(pltpu.make_async_copy(depth_all, depth_out, store_sem.at[1]))
    stores[1].start()

    def geo_body(i, carry):
        at = pl.multiple_of(i * CHUNK, SUB)
        up = smooth[pl.ds(at + SUB + 1, CHUNK), :]
        low = smooth[pl.ds(at + SUB - 1, CHUNK), :]
        grad_r = (up - low) * 0.25
        grad_c = diff_c[pl.ds(at + SUB, CHUNK), :] * 0.25
        upright = lax.rsqrt(1.0 + grad_r * grad_r + grad_c * grad_c)
        geo[0, pl.ds(at, CHUNK), :] = -grad_r * upright
        geo[1, pl.ds(at, CHUNK), :] = -grad_c * upright
        geo[2, pl.ds(at, CHUNK), :] = upright
        geo[3, pl.ds(at, CHUNK), :] = (up + low + sum_c[pl.ds(at + SUB, CHUNK), :]) * 0.25
        return carry

    lax.fori_loop(0, rows // CHUNK, geo_body, 0)
    stores.append(pltpu.make_async_copy(geo, geo_out, store_sem.at[2]))
    stores[2].start()

    for copy in block_copies:
        copy.wait()
    for copy in index_copies:
        copy.wait_send()
    for store in stores:
        store.wait()


def flow(
    tiles,
    east_hbm,
    geo_in,
    block_hbm,
    depth_hbm,
    geo_out,
    flow_out,
    east_ref,
    block_in,
    state,
    result,
    geo_held,
    load_sem,
    geo_sem,
    store_sem,
):
    t = lax.axis_index("tile")
    state_rows, width = depth_hbm.shape
    piece = state_rows - 2 * STEPS
    block_rows = block_in.shape[1]
    loads = [
        pltpu.make_async_copy(source, target, load_sem.at[n])
        for n, (source, target) in enumerate(
            ((east_hbm, east_ref), (block_hbm, block_in), (depth_hbm, state.at[0]))
        )
    ]
    for load in loads:
        load.start()
    geo_loads = [
        pltpu.make_async_copy(geo_in.at[n], geo_held.at[n], geo_sem.at[n]) for n in range(4)
    ]
    for load in geo_loads:
        load.start()
    for load in loads:
        load.wait()

    first_col = east_ref[0] - REACH
    tile_at = lax.shift_right_logical(first_col, 7)
    lane_at = jnp.bitwise_and(first_col, LANES - 1)
    lane_b = lax.broadcasted_iota(jnp.int32, (block_rows, LANES), 1)
    turned = [
        pltpu.roll(block_in[jnp.minimum(tile_at + j, tiles - 1)], LANES - lane_at, 1)
        for j in range(width // LANES + 2)
    ]
    under = jnp.concatenate(
        [
            jnp.where(lane_b < LANES - lane_at, turned[j], turned[j + 1])
            for j in range(width // LANES + 1)
        ],
        axis=1,
    )
    level = five_taps(five_taps(under, 0), 1)
    middle = shifted(level, 1, 0)
    beside = shifted(level, 1, 1)
    patch = normal_fields(
        shifted(beside, 2, 0),
        beside,
        shifted(middle, 2, 1),
        middle,
        shifted(beside, 1, 0),
    )
    patch = tuple(field[:state_rows, :width] for field in patch)
    geo_stores = []
    for n in range(4):
        geo_loads[n].wait()
        geo_stores.append(pltpu.make_async_copy(geo_held.at[n], geo_out.at[n], geo_sem.at[4 + n]))
        geo_stores[n].start()

    row = lax.broadcasted_iota(jnp.int32, (state_rows, width), 0) + (t * piece - STEPS)
    col = lax.broadcasted_iota(jnp.int32, (state_rows, width), 1)
    row_ok = jnp.logical_and(row >= 0, row < piece * tiles)
    new = first_flow_step(state[0], patch, row_ok, col)
    for n in range(3):
        state[n] = new[n]

    def flow_body(i, carry):
        new = flow_step((state[0], state[1], state[2]), patch, row_ok, col)
        for n in range(3):
            state[n] = new[n]
        return carry

    lax.fori_loop(1, STEPS, flow_body, 0)
    for n in range(3):
        result[0, n] = state[n][STEPS : STEPS + piece]
    store = pltpu.make_async_copy(result, flow_out, store_sem)
    store.start()
    store.wait()
    for copy in geo_stores:
        copy.wait()


def shards(height, trigger, snow, north, east):
    groups = lax.axis_size("grp")
    tiles = lax.axis_size("tile")
    rows, cols = height.shape
    _, piece, width = trigger.shape
    assert groups == 4 and cols == LANES and rows % (PACKS * SUB) == 0 and rows % CHUNK == 0
    block_rows = -(-(piece + 2 * STEPS + 2 * REACH) // SUB) * SUB
    span = piece * (tiles - 1) + block_rows
    state_rows = piece + 2 * STEPS
    f32 = jnp.float32
    pack_rows = rows // PACKS
    anywhere = pl.BlockSpec(memory_space=pl.ANY)
    dma = pltpu.SemaphoreType.DMA
    small = groups + 10
    mib = 1024 * 1024
    geo, blocks, depth = pl.pallas_call(
        functools.partial(exchange, groups, tiles),
        out_shape=(
            jax.ShapeDtypeStruct((4, rows, cols), f32),
            jax.ShapeDtypeStruct((tiles, block_rows, cols), f32),
            jax.ShapeDtypeStruct((state_rows, width), f32),
        ),
        in_specs=[anywhere] * 4,
        out_specs=(anywhere,) * 3,
        scratch_shapes=[
            pltpu.VMEM((rows + 2 * span, cols), f32),
            pltpu.VMEM((rows + 4 * SUB, LANES), f32),
            pltpu.VMEM((rows + 2 * SUB, LANES), f32),
            pltpu.VMEM((rows + 2 * SUB, LANES), f32),
            pltpu.VMEM((rows + 2 * SUB, LANES), f32),
            pltpu.VMEM((4, rows, cols), f32),
            pltpu.VMEM((pack_rows, LANES), f32),
            pltpu.VMEM((2, pack_rows, LANES), f32),
            pltpu.VMEM((6, SUB, LANES), f32),
            pltpu.VMEM((piece, width), f32),
            pltpu.VMEM((2, SUB, width), f32),
            pltpu.VMEM((state_rows, width), f32),
            pltpu.VMEM((groups, SUB, LANES), jnp.int32),
            pltpu.VMEM((3, span, cols), f32),
            pltpu.VMEM((3, span, cols), f32),
            pltpu.VMEM((span, cols), f32),
            pltpu.SMEM((1,), jnp.int32),
            pltpu.VMEM((1, piece, width), jnp.int32),
            pltpu.VMEM((1, piece, width), jnp.int32),
            dma((4,)),
            dma((3,)),
            dma((small,)),
            dma((small,)),
            dma((3,)),
            dma((3,)),
            dma((tiles,)),
            dma((tiles,)),
        ],
        compiler_params=pltpu.CompilerParams(
            collective_id=0, has_side_effects=True, vmem_limit_bytes=VMEM_MIB * mib
        ),
    )(north, trigger, snow, height)
    return tuple(
        pl.pallas_call(
            functools.partial(flow, tiles),
            out_shape=(
                jax.ShapeDtypeStruct((4, rows, cols), f32),
                jax.ShapeDtypeStruct((1, 3, piece, width), f32),
            ),
            in_specs=[anywhere] * 4,
            out_specs=(anywhere,) * 2,
            scratch_shapes=[
                pltpu.SMEM((1,), jnp.int32),
                pltpu.VMEM((tiles, block_rows, cols), f32),
                pltpu.VMEM((3, state_rows, width), f32),
                pltpu.VMEM((1, 3, piece, width), f32),
                pltpu.VMEM((4, rows, cols), f32),
                dma((3,)),
                dma((8,)),
                dma,
            ],
            compiler_params=pltpu.CompilerParams(vmem_limit_bytes=VMEM_MIB * mib),
        )(east, geo, blocks, depth)
    )


def solution(mesh):
    return jax.shard_map(
        shards,
        mesh=mesh,
        in_specs=(
            P("grp", "tile"),
            P("grp", "tile", None),
            P("grp", "tile", None),
            P("grp"),
            P("grp"),
        ),
        out_specs=(P(None, "grp", "tile"), P("grp", None, "tile", None)),
        check_vma=False,
    )
```

```python
import functools
import jax
import jax.numpy as jnp
from jax import lax
from jax.experimental import pallas as pl
from jax.experimental.pallas import tpu as pltpu
from jax.sharding import PartitionSpec as P

STEPS = 4
REACH = 3
LANES = 128
SUB = 8
PACKS = 16
CHUNK = 64
VMEM_MIB = 60

cell_size = 2.0
gravity = 9.81
time_step = 0.1
friction = 0.2
turbulence = 500.0
depth_floor = 0.1
speed_floor = 0.5
binomial = (0.0625, 0.25, 0.375, 0.25, 0.0625)
still_wave = (gravity * depth_floor) ** 0.5

MESH = pl.DeviceIdType.MESH


def shifted(x, by, axis):
    size = x.shape[axis]
    by = by % size
    return x if by == 0 else pltpu.roll(x, size - by, axis)


def five_taps(x, axis):
    outer = x + shifted(x, 4, axis)
    inner = shifted(x, 1, axis) + shifted(x, 3, axis)
    return binomial[0] * outer + binomial[1] * inner + binomial[2] * shifted(x, 2, axis)


def normal_fields(up, low, right, left, centre):
    grad_r = (up - low) * 0.25
    grad_c = (right - left) * 0.25
    curvature = (up + low + right + left - 4.0 * centre) * 0.25
    upright = lax.rsqrt(1.0 + grad_r * grad_r + grad_c * grad_c)
    return -grad_r * upright, -grad_c * upright, upright, curvature


def flow_step(state, patch, row_ok, col):
    depth, mom_r, mom_c = state
    width = depth.shape[1]
    inv = 1.0 / jnp.maximum(depth, depth_floor)
    u_r = mom_r * inv
    u_c = mom_c * inv
    wave = jnp.sqrt(gravity * (jnp.maximum(depth, 0.0) + depth_floor))
    pressure = 0.5 * gravity * depth * depth

    reach = jnp.abs(u_r) + wave
    bound = jnp.maximum(reach, shifted(reach, 1, 0))
    gains = []
    for q, f in (
        (depth, mom_r),
        (mom_r, mom_r * u_r + pressure),
        (mom_c, mom_c * u_r),
    ):
        face = (f + shifted(f, 1, 0)) - bound * (shifted(q, 1, 0) - q)
        gains.append(face - shifted(face, -1, 0))

    reach = jnp.abs(u_c) + wave
    last = col == width - 1
    first = col == 0
    bound = jnp.maximum(reach, jnp.where(last, still_wave, shifted(reach, 1, 1)))
    rim_bound = jnp.maximum(reach, still_wave)
    totals = []
    for gain, q, f in zip(
        gains,
        (depth, mom_r, mom_c),
        (mom_c, mom_r * u_c, mom_c * u_c + pressure),
    ):
        q_next = jnp.where(last, 0.0, shifted(q, 1, 1))
        f_next = jnp.where(last, 0.0, shifted(f, 1, 1))
        face = (f + f_next) - bound * (q_next - q)
        before = jnp.where(first, f - rim_bound * q, shifted(face, -1, 1))
        totals.append(gain + (face - before))

    return finish_step(depth, mom_r, mom_c, totals, patch, row_ok)


def finish_step(depth, mom_r, mom_c, totals, patch, row_ok):
    n_r, n_c, n_z, kappa = patch
    scale = 0.5 * time_step / cell_size
    new_depth = depth - scale * totals[0]
    push = time_step * gravity * depth
    new_r = mom_r - scale * totals[1] + push * n_r
    new_c = mom_c - scale * totals[2] + push * n_c
    inv = 1.0 / jnp.maximum(new_depth, depth_floor)
    v_r = new_r * inv
    v_c = new_c * inv
    square = v_r * v_r + v_c * v_c
    energy = square + speed_floor * speed_floor
    inv_speed = lax.rsqrt(energy)
    load = jnp.maximum(gravity * n_z + kappa * square, 0.0)
    drag = time_step * (
        friction * load * inv_speed + (gravity / turbulence) * (energy * inv_speed) * inv
    )
    damp = 1.0 / (1.0 + drag)
    return (
        jnp.where(row_ok, new_depth, 0.0),
        jnp.where(row_ok, new_r * damp, 0.0),
        jnp.where(row_ok, new_c * damp, 0.0),
    )


def first_flow_step(depth, patch, row_ok, col):
    width = depth.shape[1]
    wave = jnp.sqrt(gravity * (jnp.maximum(depth, 0.0) + depth_floor))
    pressure = 0.5 * gravity * depth * depth

    bound = jnp.maximum(wave, shifted(wave, 1, 0))
    face = bound * (depth - shifted(depth, 1, 0))
    gain = face - shifted(face, -1, 0)
    gain_r = shifted(pressure, 1, 0) - shifted(pressure, -1, 0)

    last = col == width - 1
    first = col == 0
    bound = jnp.maximum(wave, jnp.where(last, still_wave, shifted(wave, 1, 1)))
    face = bound * (depth - jnp.where(last, 0.0, shifted(depth, 1, 1)))
    before = jnp.where(first, -jnp.maximum(wave, still_wave) * depth, shifted(face, -1, 1))
    gain = gain + (face - before)
    gain_c = jnp.where(last, 0.0, shifted(pressure, 1, 1)) - jnp.where(
        first, 0.0, shifted(pressure, -1, 1)
    )
    return finish_step(depth, 0.0, 0.0, (gain, gain_r, gain_c), patch, row_ok)


def exchange(
    groups,
    tiles,
    north_hbm,
    trigger_hbm,
    snow_hbm,
    height_hbm,
    geo_out,
    block_out,
    depth_out,
    high,
    side,
    smooth,
    diff_c,
    sum_c,
    geo,
    packed,
    packed_in,
    edge_in,
    depth_own,
    depth_in,
    depth_all,
    index,
    strip_out,
    strip_in,
    strip,
    north_ref,
    trigger_ref,
    snow_ref,
    load_sem,
    store_sem,
    send_sem,
    recv_sem,
    strip_send,
    strip_recv,
    block_send,
    block_recv,
):
    g = lax.axis_index("grp")
    t = lax.axis_index("tile")
    rows = height_hbm.shape[0]
    piece = trigger_hbm.shape[1]
    width = trigger_hbm.shape[2]
    span = strip.shape[0]
    block_rows = block_out.shape[1]
    window_rows = piece * tiles
    pad = span
    state_rows = piece + 2 * STEPS
    north_of = lambda d: lax.rem(g + d + groups, groups)
    east_of = lambda d: lax.rem(t + d + tiles, tiles)
    other = g + 1 - 2 * lax.rem(g, 2)
    across = lax.rem(g + 2, groups)
    across_other = lax.rem(other + 2, groups)

    loads = [
        pltpu.make_async_copy(source, target, load_sem.at[n])
        for n, (source, target) in enumerate(
            (
                (north_hbm, north_ref),
                (height_hbm, high.at[pl.ds(pad, rows)]),
                (trigger_hbm, trigger_ref),
                (snow_hbm, snow_ref),
            )
        )
    ]
    for load in loads:
        load.start()

    barrier = pltpu.get_barrier_semaphore()
    peers = (
        [(other, t), (across, t), (across_other, t)]
        + [(g, east_of(d)) for d in range(1, tiles)]
        + [(north_of(a), east_of(b)) for a in (-1, 1) for b in (-1, 1)]
    )
    for peer in peers:
        pl.semaphore_signal(barrier, inc=1, device_id=peer, device_id_type=MESH)

    lane8 = lax.broadcasted_iota(jnp.int32, (SUB, LANES), 1)
    loads[0].wait()
    r0 = north_ref[0]
    index[0] = jnp.zeros((SUB, LANES), jnp.int32) + r0
    zeros = jnp.zeros((pad, LANES), jnp.float32)
    high[pl.ds(0, pad), :] = zeros
    high[pl.ds(pad + rows, pad), :] = zeros
    loads[2].wait()
    loads[3].wait()
    own_depth = (
        trigger_ref[0].astype(jnp.float32) * snow_ref[0].astype(jnp.float32) * 0.01
    )
    depth_own[...] = own_depth

    loads[1].wait()
    pack_rows = rows // PACKS
    lane_p = lax.broadcasted_iota(jnp.int32, (pack_rows, LANES), 1)
    step = LANES // PACKS
    total = jnp.zeros((pack_rows, LANES), jnp.float32)
    for k in range(PACKS):
        part = high[pl.ds(pad + k * pack_rows, pack_rows), :]
        both = jnp.where(lane_p < step // 2, part, pltpu.roll(part, step, 1))
        if k:
            both = pltpu.roll(both, step * k, 1)
        total = jnp.where(lane_p // step == k, both, total)
    packed[...] = total

    pl.semaphore_wait(barrier, len(peers))

    def remote(src, dst, sends, recvs, slot, peer):
        return pltpu.make_async_remote_copy(
            src_ref=src,
            dst_ref=dst,
            send_sem=sends.at[slot],
            recv_sem=recvs.at[slot],
            device_id=peer,
            device_id_type=MESH,
        )

    index_copies = [
        remote(index.at[0], index.at[d], send_sem, recv_sem, d - 1, (peer, t))
        for d, peer in ((3, across_other), (2, across), (1, other))
    ]
    lower = high.at[pl.ds(pad, SUB)]
    upper = high.at[pl.ds(pad + rows - SUB, SUB)]
    base = groups + 6
    halo_copies = [
        remote(packed, packed_in.at[0], send_sem, recv_sem, base + 2, (g, east_of(1))),
        remote(packed, packed_in.at[1], send_sem, recv_sem, base + 3, (g, east_of(-1))),
    ]
    for b in (-1, 0, 1):
        halo_copies.append(
            remote(upper, edge_in.at[1 - b], send_sem, recv_sem, groups + 1 - b, (north_of(1), east_of(b)))
        )
        halo_copies.append(
            remote(lower, edge_in.at[4 - b], send_sem, recv_sem, groups + 4 - b, (north_of(-1), east_of(b)))
        )
    depth_copies = [
        remote(depth_own.at[pl.ds(piece - SUB, SUB)], depth_in.at[0], send_sem, recv_sem, base, (g, east_of(1))),
        remote(depth_own.at[pl.ds(0, SUB)], depth_in.at[1], send_sem, recv_sem, base + 1, (g, east_of(-1))),
    ]
    for copy in index_copies + halo_copies + depth_copies:
        copy.start()

    def part_of(first):
        start = jnp.clip(first - (REACH + STEPS) - g * rows, -pad, rows) + pad
        return high[pl.ds(start, span), :]

    index_copies[0].wait_recv()
    strip_out[0] = part_of(index[3][0, 0])
    far = remote(strip_out.at[0], strip_in.at[0], strip_send, strip_recv, 0, (other, t))
    far.start()
    index_copies[1].wait_recv()
    first_across = index[2][0, 0]
    strip_out[2] = part_of(first_across)

    row_in = lax.broadcasted_iota(jnp.int32, (span, LANES), 0) - (REACH + STEPS)

    def of_block(first, block):
        return jnp.logical_and(row_in >= block * rows - first, row_in < (block + 1) * rows - first)

    far.wait()
    strip_out[2] = jnp.where(of_block(first_across, other), strip_in[0], strip_out[2])
    long = remote(strip_out.at[2], strip_in.at[2], strip_send, strip_recv, 2, (across, t))
    long.start()
    index_copies[2].wait_recv()
    strip_out[1] = part_of(index[1][0, 0])
    near = remote(strip_out.at[1], strip_in.at[1], strip_send, strip_recv, 1, (other, t))
    near.start()
    strip[...] = part_of(r0)

    for copy in halo_copies:
        copy.wait()

    has_above = g > 0
    has_below = g < groups - 1
    has_left = t > 0
    has_right = t < tiles - 1
    right_half = lane8 < LANES // 2
    for at, slot, here in (
        (pad - SUB, 0, has_above),
        (pad + rows, 3, has_below),
    ):
        high[pl.ds(at, SUB), :] = jnp.where(here, edge_in[slot + 1], 0.0)
        right = jnp.where(jnp.logical_and(here, has_right), edge_in[slot + 2], 0.0)
        left = jnp.where(jnp.logical_and(here, has_left), edge_in[slot], 0.0)
        side[pl.ds(at - pad + 2 * SUB, SUB), :] = jnp.where(right_half, right, left)
    side[pl.ds(0, SUB), :] = jnp.zeros((SUB, LANES), jnp.float32)
    side[pl.ds(rows + 3 * SUB, SUB), :] = jnp.zeros((SUB, LANES), jnp.float32)
    right = jnp.where(has_right, packed_in[1], 0.0)
    left = jnp.where(has_left, packed_in[0], 0.0)
    mixed = jnp.where(lane_p % step < step // 2, right, left)
    for k in range(PACKS):
        ahead = shifted(mixed, step * k, 1)
        behind = shifted(mixed, step * k + step, 1)
        side[pl.ds(2 * SUB + k * pack_rows, pack_rows), :] = jnp.where(
            lane_p < LANES // 2, ahead, behind
        )

    def smooth_rows(at, count):
        def down(ref, offset):
            o = at + offset
            return (
                binomial[0] * (ref[pl.ds(o - 2, count), :] + ref[pl.ds(o + 2, count), :])
                + binomial[1] * (ref[pl.ds(o - 1, count), :] + ref[pl.ds(o + 1, count), :])
                + binomial[2] * ref[pl.ds(o, count), :]
            )

        both = jnp.concatenate([down(high, pad - SUB), down(side, SUB)], axis=1)
        both = (
            binomial[0] * (shifted(both, -2, 1) + shifted(both, 2, 1))
            + binomial[1] * (shifted(both, -1, 1) + shifted(both, 1, 1))
            + binomial[2] * both
        )
        centre = both[:, :LANES]
        right = shifted(both, 1, 1)[:, :LANES]
        left = shifted(both, -1, 1)[:, :LANES]
        smooth[pl.ds(at, count), :] = centre
        diff_c[pl.ds(at, count), :] = right - left
        sum_c[pl.ds(at, count), :] = right + left - 4.0 * centre

    smooth_rows(0, SUB)
    smooth_rows(rows + SUB, SUB)

    def smooth_body(i, carry):
        smooth_rows(pl.multiple_of(SUB + i * CHUNK, SUB), CHUNK)
        return carry

    lax.fori_loop(0, rows // CHUNK, smooth_body, 0)

    near.wait()
    long.wait()
    strip[...] = jnp.where(
        of_block(r0, g),
        strip[...],
        jnp.where(of_block(r0, other), strip_in[1], strip_in[2]),
    )
    block_copies = []
    for d in range(1, tiles):
        to = east_of(d)
        copy = remote(
            strip.at[pl.ds(pl.multiple_of(to * piece, SUB), block_rows)],
            block_out.at[t],
            block_send,
            block_recv,
            d,
            (g, to),
        )
        copy.start()
        block_copies.append(copy)
    stores = [
        pltpu.make_async_copy(
            strip.at[pl.ds(pl.multiple_of(t * piece, SUB), block_rows)],
            block_out.at[t],
            store_sem.at[0],
        )
    ]
    stores[0].start()

    for copy in depth_copies:
        copy.wait()
    row = lax.broadcasted_iota(jnp.int32, (state_rows, width), 0) + (t * piece - STEPS)
    row_ok = jnp.logical_and(row >= 0, row < window_rows)
    depth = jnp.concatenate(
        [depth_in[0][SUB - STEPS :], depth_own[...], depth_in[1][:STEPS]], axis=0
    )
    depth_all[...] = jnp.where(row_ok, depth, 0.0)
    stores.append(pltpu.make_async_copy(depth_all, depth_out, store_sem.at[1]))
    stores[1].start()

    def geo_body(i, carry):
        at = pl.multiple_of(i * CHUNK, SUB)
        up = smooth[pl.ds(at + SUB + 1, CHUNK), :]
        low = smooth[pl.ds(at + SUB - 1, CHUNK), :]
        grad_r = (up - low) * 0.25
        grad_c = diff_c[pl.ds(at + SUB, CHUNK), :] * 0.25
        upright = lax.rsqrt(1.0 + grad_r * grad_r + grad_c * grad_c)
        geo[0, pl.ds(at, CHUNK), :] = -grad_r * upright
        geo[1, pl.ds(at, CHUNK), :] = -grad_c * upright
        geo[2, pl.ds(at, CHUNK), :] = upright
        geo[3, pl.ds(at, CHUNK), :] = (up + low + sum_c[pl.ds(at + SUB, CHUNK), :]) * 0.25
        return carry

    lax.fori_loop(0, rows // CHUNK, geo_body, 0)
    stores.append(pltpu.make_async_copy(geo, geo_out, store_sem.at[2]))
    stores[2].start()

    for copy in block_copies:
        copy.wait()
    for copy in index_copies:
        copy.wait_send()
    for store in stores:
        store.wait()


def flow(
    tiles,
    east_hbm,
    geo_in,
    block_hbm,
    depth_hbm,
    geo_out,
    flow_out,
    east_ref,
    block_in,
    state,
    result,
    geo_held,
    load_sem,
    geo_sem,
    store_sem,
):
    t = lax.axis_index("tile")
    state_rows, width = depth_hbm.shape
    piece = state_rows - 2 * STEPS
    block_rows = block_in.shape[1]
    loads = [
        pltpu.make_async_copy(source, target, load_sem.at[n])
        for n, (source, target) in enumerate(
            ((east_hbm, east_ref), (block_hbm, block_in), (depth_hbm, state.at[0]))
        )
    ]
    for load in loads:
        load.start()
    geo_loads = [
        pltpu.make_async_copy(geo_in.at[n], geo_held.at[n], geo_sem.at[n]) for n in range(4)
    ]
    for load in geo_loads:
        load.start()
    for load in loads:
        load.wait()

    first_col = east_ref[0] - REACH
    tile_at = lax.shift_right_logical(first_col, 7)
    lane_at = jnp.bitwise_and(first_col, LANES - 1)
    lane_b = lax.broadcasted_iota(jnp.int32, (block_rows, LANES), 1)
    turned = [
        pltpu.roll(block_in[jnp.minimum(tile_at + j, tiles - 1)], LANES - lane_at, 1)
        for j in range(width // LANES + 2)
    ]
    under = jnp.concatenate(
        [
            jnp.where(lane_b < LANES - lane_at, turned[j], turned[j + 1])
            for j in range(width // LANES + 1)
        ],
        axis=1,
    )
    level = five_taps(five_taps(under, 0), 1)
    middle = shifted(level, 1, 0)
    beside = shifted(level, 1, 1)
    patch = normal_fields(
        shifted(beside, 2, 0),
        beside,
        shifted(middle, 2, 1),
        middle,
        shifted(beside, 1, 0),
    )
    patch = tuple(field[:state_rows, :width] for field in patch)
    geo_stores = []
    for n in range(4):
        geo_loads[n].wait()
        geo_stores.append(pltpu.make_async_copy(geo_held.at[n], geo_out.at[n], geo_sem.at[4 + n]))
        geo_stores[n].start()

    row = lax.broadcasted_iota(jnp.int32, (state_rows, width), 0) + (t * piece - STEPS)
    col = lax.broadcasted_iota(jnp.int32, (state_rows, width), 1)
    row_ok = jnp.logical_and(row >= 0, row < piece * tiles)
    new = first_flow_step(state[0], patch, row_ok, col)
    for n in range(3):
        state[n] = new[n]

    def flow_body(i, carry):
        new = flow_step((state[0], state[1], state[2]), patch, row_ok, col)
        for n in range(3):
            state[n] = new[n]
        return carry

    lax.fori_loop(1, STEPS, flow_body, 0)
    for n in range(3):
        result[0, n] = state[n][STEPS : STEPS + piece]
    store = pltpu.make_async_copy(result, flow_out, store_sem)
    store.start()
    store.wait()
    for copy in geo_stores:
        copy.wait()


def shards(height, trigger, snow, north, east):
    groups = lax.axis_size("grp")
    tiles = lax.axis_size("tile")
    rows, cols = height.shape
    _, piece, width = trigger.shape
    assert groups == 4 and cols == LANES and rows % (PACKS * SUB) == 0 and rows % CHUNK == 0
    block_rows = -(-(piece + 2 * STEPS + 2 * REACH) // SUB) * SUB
    span = piece * (tiles - 1) + block_rows
    state_rows = piece + 2 * STEPS
    f32 = jnp.float32
    pack_rows = rows // PACKS
    anywhere = pl.BlockSpec(memory_space=pl.ANY)
    dma = pltpu.SemaphoreType.DMA
    small = groups + 10
    mib = 1024 * 1024
    geo, blocks, depth = pl.pallas_call(
        functools.partial(exchange, groups, tiles),
        out_shape=(
            jax.ShapeDtypeStruct((4, rows, cols), f32),
            jax.ShapeDtypeStruct((tiles, block_rows, cols), f32),
            jax.ShapeDtypeStruct((state_rows, width), f32),
        ),
        in_specs=[anywhere] * 4,
        out_specs=(anywhere,) * 3,
        scratch_shapes=[
            pltpu.VMEM((rows + 2 * span, cols), f32),
            pltpu.VMEM((rows + 4 * SUB, LANES), f32),
            pltpu.VMEM((rows + 2 * SUB, LANES), f32),
            pltpu.VMEM((rows + 2 * SUB, LANES), f32),
            pltpu.VMEM((rows + 2 * SUB, LANES), f32),
            pltpu.VMEM((4, rows, cols), f32),
            pltpu.VMEM((pack_rows, LANES), f32),
            pltpu.VMEM((2, pack_rows, LANES), f32),
            pltpu.VMEM((6, SUB, LANES), f32),
            pltpu.VMEM((piece, width), f32),
            pltpu.VMEM((2, SUB, width), f32),
            pltpu.VMEM((state_rows, width), f32),
            pltpu.VMEM((groups, SUB, LANES), jnp.int32),
            pltpu.VMEM((3, span, cols), f32),
            pltpu.VMEM((3, span, cols), f32),
            pltpu.VMEM((span, cols), f32),
            pltpu.SMEM((1,), jnp.int32),
            pltpu.VMEM((1, piece, width), jnp.int32),
            pltpu.VMEM((1, piece, width), jnp.int32),
            dma((4,)),
            dma((3,)),
            dma((small,)),
            dma((small,)),
            dma((3,)),
            dma((3,)),
            dma((tiles,)),
            dma((tiles,)),
        ],
        compiler_params=pltpu.CompilerParams(
            collective_id=0, has_side_effects=True, vmem_limit_bytes=VMEM_MIB * mib
        ),
    )(north, trigger, snow, height)
    return tuple(
        pl.pallas_call(
            functools.partial(flow, tiles),
            out_shape=(
                jax.ShapeDtypeStruct((4, rows, cols), f32),
                jax.ShapeDtypeStruct((1, 3, piece, width), f32),
            ),
            in_specs=[anywhere] * 4,
            out_specs=(anywhere,) * 2,
            scratch_shapes=[
                pltpu.SMEM((1,), jnp.int32),
                pltpu.VMEM((tiles, block_rows, cols), f32),
                pltpu.VMEM((3, state_rows, width), f32),
                pltpu.VMEM((1, 3, piece, width), f32),
                pltpu.VMEM((4, rows, cols), f32),
                dma((3,)),
                dma((8,)),
                dma,
            ],
            compiler_params=pltpu.CompilerParams(vmem_limit_bytes=VMEM_MIB * mib),
        )(east, geo, blocks, depth)
    )


def solution(mesh):
    return jax.shard_map(
        shards,
        mesh=mesh,
        in_specs=(
            P("grp", "tile"),
            P("grp", "tile", None),
            P("grp", "tile", None),
            P("grp"),
            P("grp"),
        ),
        out_specs=(P(None, "grp", "tile"), P("grp", None, "tile", None)),
        check_vma=False,
    )
```
